256 devices in a mesh: blk: 64 (over z, x, core), rep: 4 (over y).
Axes of the slice: x: 4, y: 4, z: 8, core: 2. Of those that a mesh axis runs over, the one named last changes fastest.
Arguments:
- embeddings: float32 [192, 1024, 1024], P('blk')
- pairs: int32 [192, 6], P('blk'), may hold values from 0 to 1, as said below
Outputs:
- best: float32 [192, 1024], P('blk')
The draws below stay inside these ranges and needn't reach their ends.
Inputs may be any that keep to these rules, and one draw needn't show every extreme that they name: pairs[i, k - 1] is 0 where i + k >= 192; some block lies in no listed pair.
All inputs are finite; a program needn't handle non-finite values.
Results may differ from the reference program's by a relative error of at most 0.0003.
Values may be sent and summed in bfloat16 or wider, within the bound.
A program may use at most 128 MiB of HBM per device.

```python
import jax
import jax.numpy as jnp
from jax import lax

D = 1024
R = 1024
REACH = 6
NB = 192


def listed_pairs(key):
    key_draw, key_lone, key_pick = jax.random.split(key, 3)
    values = jax.random.randint(key_draw, (NB, REACH), 0, 10)
    offsets = jnp.arange(REACH, dtype=jnp.int32)[None, :] + 1
    blocks = jnp.arange(NB, dtype=jnp.int32)[:, None]
    ceiling = 9 - 5 * (offsets - 1) // max(REACH - 1, 1)
    lonely = jax.random.randint(key_lone, (NB,), 0, 10) == 0
    forced = jax.random.randint(key_pick, (), 0, NB)
    lonely = jnp.logical_or(lonely, jnp.arange(NB, dtype=jnp.int32) == forced)
    partner = jnp.minimum(blocks + offsets, NB - 1)
    listed = values < ceiling
    listed = jnp.logical_and(listed, blocks + offsets < NB)
    listed = jnp.logical_and(listed, jnp.logical_not(lonely)[:, None])
    listed = jnp.logical_and(listed, jnp.logical_not(lonely[partner]))
    return listed.astype(jnp.int32)


def draw_pairs(key, part):
    return listed_pairs(key)


def draw_embeddings(key, part):
    listed = listed_pairs(key)
    key = jax.random.fold_in(key, 11)
    key_noise = jax.random.fold_in(key, 0)
    key_choose = jax.random.fold_in(key, 3)
    key_row = jax.random.fold_in(key, 4)
    key_weight = jax.random.fold_in(key, 5)
    noise = jax.random.normal(key_noise, (NB, R, D), jnp.float32)
    scores = jax.random.randint(key_choose, (NB, R, REACH), 1, 1 << 20)
    scores = jnp.where(listed[:, None, :] == 1, scores, 0)
    offset = jnp.argmax(scores, axis=2).astype(jnp.int32) + 1
    planted = jnp.max(scores, axis=2) > 0
    blocks = jnp.arange(NB, dtype=jnp.int32)[:, None]
    target = jnp.minimum(blocks + offset, NB - 1)
    chosen_rows = jax.random.randint(key_row, (NB, R), 0, R)
    flat_noise = noise.reshape(NB * R, D)
    partner = flat_noise[(target * R + chosen_rows).reshape(-1)].reshape(NB, R, D)
    weight = jax.random.uniform(key_weight, (NB, R, 1), jnp.float32, 1.0, 3.0)
    weight = jnp.where(planted[:, :, None], weight, 0.0)
    return (noise + weight * partner).astype(jnp.float32)


def setup_inputs(seed: int = 0) -> dict:
    seeds = jax.random.split(jax.random.key(seed), 3)
    return {
        "embeddings": draw_embeddings(jax.random.fold_in(seeds[2], 71), 0),
        "pairs": draw_pairs(jax.random.fold_in(seeds[2], 71), 0),
    }


def reference(embeddings, pairs):
    squares = lax.optimization_barrier(jnp.sum(embeddings * embeddings, axis=2, keepdims=True))
    unit = (embeddings / jnp.sqrt(squares + 1e-06)).astype(jnp.bfloat16)
    nblocks = unit.shape[0]
    reach = pairs.shape[1]
    start = jnp.full(unit.shape[:2], -1.0, jnp.float32)

    def visit(index, best):
        index = jnp.asarray(index).astype(jnp.int32)
        first = index // reach
        offset = index % reach + 1
        second = jnp.minimum(first + offset, nblocks - 1).astype(jnp.int32)

        def tile(current):
            left = lax.dynamic_index_in_dim(unit, first, 0, keepdims=False)
            right = lax.dynamic_index_in_dim(unit, second, 0, keepdims=False)
            sim = lax.dot_general(left, right, (((1,), (1,)), ((), ())), preferred_element_type=jnp.float32)
            current = current.at[first].max(lax.optimization_barrier(jnp.max(sim, axis=1)))
            return current.at[second].max(lax.optimization_barrier(jnp.max(sim, axis=0)))
        listed = pairs[first, offset - 1] == 1
        return lax.cond(listed, tile, lambda current: current, best)
    return lax.fori_loop(0, nblocks * reach, visit, start)
```

```python
import jax
import jax.numpy as jnp
from jax import lax
from jax.experimental import pallas as pl
from jax.experimental.pallas import tpu as pltpu
from jax.sharding import PartitionSpec as P

MESH = pl.DeviceIdType.MESH
REP = 4
PIECES = 4
LANES = 256
NT = (((1,), (1,)), ((), ()))


def fold_lanes(sim):
    out = sim[:, :128]
    for j in range(1, sim.shape[1] // 128):
        out = jnp.maximum(out, sim[:, 128 * j : 128 * (j + 1)])
    return out


def fold_rows(sim):
    return jnp.max(sim.reshape(-1, 8, sim.shape[1]), axis=0)


def kernel(
    places,
    emb,
    pairs,
    out,
    stage,
    own,
    mine,
    near,
    far,
    row_max,
    pairs_here,
    pairs_there,
    pairs_far,
    pairs_far_s,
    msg_row,
    msg_near,
    msg_far,
    got_row,
    got_near,
    got_far,
    load_sem,
    pair_sem,
    far_send,
    far_recv,
    near_send,
    near_recv,
    end_send,
    row_recv,
    got_near_recv,
    got_far_recv,
):
    blocks, rows, width = own.shape
    quarter = rows // REP
    piece = quarter // PIECES
    count = blocks * PIECES
    place = lax.axis_index("blk")
    y = lax.axis_index("rep")
    core = lax.rem(place, 2)
    first = core == 0

    def phys(o):
        return jnp.where(first, o, blocks - 1 - o)

    def at(distance):
        return lax.rem(place + distance + places, places)

    sibling = place + 1 - 2 * core
    sends_to = jnp.where(first, at(-2), at(2))
    gets_from = jnp.where(first, at(2), at(-2))

    def piece_rows(i):
        return pl.ds(pl.multiple_of(y * quarter + (i % PIECES) * piece, piece), piece)

    loads = []
    for i in range(count):
        o = i // PIECES
        loads.append(
            pltpu.make_async_copy(
                emb.at[phys(o), piece_rows(i), :],
                stage.at[o, piece_rows(i), :],
                load_sem.at[i],
            )
        )
    rest = []
    for j in range(1, REP):
        span = pl.ds(pl.multiple_of(lax.rem(y + j, REP) * quarter, quarter), quarter)
        for o in range(blocks):
            rest.append((o, span))
            loads.append(
                pltpu.make_async_copy(
                    emb.at[phys(o), span, :],
                    stage.at[o, span, :],
                    load_sem.at[count + len(rest) - 1],
                )
            )
    for load in loads:
        load.start()
    pairs_load = pltpu.make_async_copy(pairs, pairs_there, pair_sem.at[0])
    pairs_load.start()
    pairs_load_s = pltpu.make_async_copy(pairs, pairs_here, pair_sem.at[1])
    pairs_load_s.start()

    barrier = pltpu.get_barrier_semaphore()
    others = [{"rep": lax.rem(y + j, REP)} for j in range(1, REP)]
    others += [
        {"blk": at(d), "rep": lax.rem(y + j, REP)}
        for d in (-2, 2, -1, 1)
        for j in range(REP)
    ]
    for other in others:
        pl.semaphore_signal(barrier, inc=1, device_id=other, device_id_type=MESH)
    row_max[...] = jnp.full(row_max.shape, -1.0, jnp.float32)
    pl.semaphore_wait(barrier, len(others))

    def unit(block):
        squares = jnp.sum(block * block, axis=1, keepdims=True)
        return (block * lax.rsqrt(squares + 1e-06)).astype(jnp.bfloat16)

    def part(i):
        return pl.ds((i % PIECES) * piece, piece)

    def far_copy(i):
        return pltpu.make_async_remote_copy(
            src_ref=mine.at[i // PIECES, part(i), :],
            dst_ref=far.at[i // PIECES, part(i), :],
            send_sem=far_send.at[i],
            recv_sem=far_recv.at[i],
            device_id={"blk": sends_to},
            device_id_type=MESH,
        )

    def near_copy(i, source):
        return pltpu.make_async_remote_copy(
            src_ref=source.at[i // PIECES, part(i), :],
            dst_ref=near.at[i // PIECES, part(i), :],
            send_sem=near_send.at[i],
            recv_sem=near_recv.at[i],
            device_id={"blk": sibling},
            device_id_type=MESH,
        )

    for i in range(count):
        o = i // PIECES
        loads[i].wait()
        value = unit(stage[o, piece_rows(i), :])
        mine[o, part(i), :] = value
        own[o, piece_rows(i), :] = value
        far_copy(i).start()

        @pl.when(core == 1)
        def _():
            near_copy(i, mine).start()

    pairs_load.wait()
    pairs_load_s.wait()
    pairs_copy = pltpu.make_async_remote_copy(
        src_ref=pairs_there,
        dst_ref=pairs_far,
        send_sem=pair_sem.at[2],
        recv_sem=pair_sem.at[3],
        device_id={"blk": at(2)},
        device_id_type=MESH,
    )
    pairs_copy.start()
    for n, (o, span) in enumerate(rest):
        loads[count + n].wait()
        own[o, span, :] = unit(stage[o, span, :])

    pairs_copy.wait()
    pairs_move = pltpu.make_async_copy(pairs_far, pairs_far_s, pair_sem.at[4])
    pairs_move.start()
    pairs_move.wait()

    def cap(listed):
        return listed.astype(jnp.float32) * 1e30 - 1.0

    def own_cap(o1, o2):
        return cap(pairs_here[jnp.where(first, o1, blocks - 1 - o2), o2 - o1 - 1])

    def near_cap(o, q):
        return cap(
            pairs_here[
                jnp.where(first, o, blocks - 1 - o),
                jnp.where(first, 2 * blocks - 2 - q - o, o + q),
            ]
        )

    def far_cap(o, q):
        here = pairs_here[o, 2 * blocks - 1 + q - o]
        there = pairs_far_s[blocks - 1 - q, 2 * blocks - 1 + q - o]
        return cap(jnp.where(first, here, there))

    def multiply(left, targets):
        kept = None
        for o, limit in targets:
            mine_max = None
            for c in range(rows // LANES):
                lanes = pl.ds(c * LANES, LANES)
                sim = lax.dot_general(
                    left, own[o, lanes, :], NT, preferred_element_type=jnp.float32
                )
                down = jnp.minimum(fold_rows(sim), limit)
                row_max[o, :, lanes] = jnp.maximum(row_max[o, :, lanes], down)
                across = fold_lanes(sim)
                mine_max = across if mine_max is None else jnp.maximum(mine_max, across)
            mine_max = jnp.minimum(mine_max, limit)
            kept = mine_max if kept is None else jnp.maximum(kept, mine_max)
        turned = [
            jnp.max(kept[128 * j : 128 * (j + 1), :].T, axis=0, keepdims=True)
            for j in range(quarter // 128)
        ]
        return jnp.concatenate(turned, axis=1)

    msg_row[...] = jnp.full(msg_row.shape, -1.0, jnp.float32)
    lanes_here = pl.ds(pl.multiple_of(y * quarter, quarter), quarter)
    for q in range(blocks - 1):
        targets = [(o, own_cap(q, o)) for o in range(q + 1, blocks)]
        msg_row[q, :, lanes_here] = multiply(mine[q], targets)

    def near_tiles(q):
        targets = [(o, near_cap(o, q)) for o in range(blocks)]
        msg_near[q] = multiply(near[q], targets)

    def far_tiles(q):
        targets = [(o, far_cap(o, q)) for o in range(q, blocks)]
        msg_far[q] = multiply(far[q], targets)

    @pl.when(core == 0)
    def _():
        def relay(i):
            far_copy(i).wait_recv()
            near_copy(i, far).start()

        half = PIECES // 2
        for q in range(blocks):
            for i in range(half):
                relay(q * PIECES + i)
            for i in range(PIECES):
                near_copy(q * PIECES + i, far).wait_recv()
            near_tiles(q)
            for i in range(half, PIECES):
                relay(q * PIECES + i)
            far_tiles(q)

    @pl.when(core == 1)
    def _():
        for q in range(blocks):
            for i in range(PIECES):
                far_copy(q * PIECES + i).wait_recv()
            far_tiles(q)
            for i in range(PIECES):
                near_copy(q * PIECES + i, mine).wait_recv()
            near_tiles(q)

    for o in range(blocks):
        msg_row[o] = jnp.maximum(msg_row[o], jnp.max(row_max[o], axis=0, keepdims=True))

    def end_copy(k, source, target, recv, blk, rep):
        return pltpu.make_async_remote_copy(
            src_ref=source,
            dst_ref=target.at[y],
            send_sem=end_send.at[k],
            recv_sem=recv.at[y],
            device_id={"blk": blk, "rep": rep},
            device_id_type=MESH,
        )

    ends = []
    for j in range(REP):
        rep = lax.rem(y + j, REP)
        ends.append(end_copy(3 * j, msg_near, got_near, got_near_recv, at(1), rep))
        ends.append(end_copy(3 * j + 1, msg_far, got_far, got_far_recv, gets_from, rep))
        if j:
            ends.append(end_copy(3 * j + 2, msg_row, got_row, row_recv, place, rep))
    for copy in ends:
        copy.start()

    def arrived(source, target, recv, slot):
        pltpu.make_async_remote_copy(
            src_ref=source,
            dst_ref=target.at[slot],
            send_sem=end_send.at[0],
            recv_sem=recv.at[slot],
            device_id={"blk": place, "rep": lax.rem(y + 1, REP)},
            device_id_type=MESH,
        ).wait_recv()

    for j in range(REP):
        slot = lax.rem(y + j, REP)
        arrived(msg_near, got_near, got_near_recv, slot)
        arrived(msg_far, got_far, got_far_recv, slot)
        if j:
            arrived(msg_row, got_row, row_recv, slot)

    best = []
    for o in range(blocks):
        value = msg_row[o]
        for j in range(1, REP):
            value = jnp.maximum(value, got_row[lax.rem(y + j, REP), o])
        side = [jnp.maximum(got_near[j, o], got_far[j, o]) for j in range(REP)]
        best.append(jnp.maximum(value, jnp.concatenate(side, axis=1)))
    for o in range(blocks):
        out[o : o + 1, :] = jnp.where(first, best[o], best[blocks - 1 - o])

    for copy in ends:
        copy.wait_send()
    for i in range(count):
        far_copy(i).wait_send()
        near_copy(i, mine).wait_send()


def solution(mesh):
    places = mesh.shape["blk"]

    def per_device(embeddings, pairs):
        blocks, rows, width = embeddings.shape
        reach = pairs.shape[1]
        quarter = rows // REP
        count = blocks * PIECES
        dma = pltpu.SemaphoreType.DMA

        def body(*refs):
            kernel(places, *refs)

        return pl.pallas_call(
            body,
            out_shape=jax.ShapeDtypeStruct((blocks, rows), jnp.float32),
            in_specs=[pl.BlockSpec(memory_space=pltpu.HBM)] * 2,
            out_specs=pl.BlockSpec(memory_space=pltpu.VMEM),
            scratch_shapes=[
                pltpu.VMEM((blocks, rows, width), jnp.float32),
                pltpu.VMEM((blocks, rows, width), jnp.bfloat16),
                pltpu.VMEM((blocks, quarter, width), jnp.bfloat16),
                pltpu.VMEM((blocks, quarter, width), jnp.bfloat16),
                pltpu.VMEM((blocks, quarter, width), jnp.bfloat16),
                pltpu.VMEM((blocks, 8, rows), jnp.float32),
                pltpu.SMEM((blocks, reach), jnp.int32),
                pltpu.VMEM((blocks, reach), jnp.int32),
                pltpu.VMEM((blocks, reach), jnp.int32),
                pltpu.SMEM((blocks, reach), jnp.int32),
                pltpu.VMEM((blocks, 1, rows), jnp.float32),
                pltpu.VMEM((blocks, 1, quarter), jnp.float32),
                pltpu.VMEM((blocks, 1, quarter), jnp.float32),
                pltpu.VMEM((REP, blocks, 1, rows), jnp.float32),
                pltpu.VMEM((REP, blocks, 1, quarter), jnp.float32),
                pltpu.VMEM((REP, blocks, 1, quarter), jnp.float32),
                dma((count + (REP - 1) * blocks,)),
                dma((5,)),
                dma((count,)),
                dma((count,)),
                dma((count,)),
                dma((count,)),
                dma((3 * REP,)),
                dma((REP,)),
                dma((REP,)),
                dma((REP,)),
            ],
            compiler_params=pltpu.CompilerParams(
                collective_id=0, has_side_effects=True, vmem_limit_bytes=56 << 20
            ),
            name="neighbours",
        )(embeddings, pairs)

    return jax.shard_map(
        per_device,
        mesh=mesh,
        in_specs=(P("blk", None, None), P("blk", None)),
        out_specs=P("blk", None),
        check_vma=False,
    )
```

```python
import jax
import jax.numpy as jnp
from jax import lax
from jax.experimental import pallas as pl
from jax.experimental.pallas import tpu as pltpu
from jax.sharding import PartitionSpec as P

MESH = pl.DeviceIdType.MESH
REP = 4
PIECES = 4
LANES = 256
NT = (((1,), (1,)), ((), ()))


def fold_lanes(sim):
    out = sim[:, :128]
    for j in range(1, sim.shape[1] // 128):
        out = jnp.maximum(out, sim[:, 128 * j : 128 * (j + 1)])
    return out


def fold_rows(sim):
    return jnp.max(sim.reshape(-1, 8, sim.shape[1]), axis=0)


def kernel(
    places,
    emb,
    pairs,
    out,
    stage,
    own,
    mine,
    near,
    far,
    row_max,
    pairs_here,
    pairs_there,
    pairs_far,
    pairs_far_s,
    msg_row,
    msg_near,
    msg_far,
    got_row,
    got_near,
    got_far,
    load_sem,
    pair_sem,
    far_send,
    far_recv,
    near_send,
    near_recv,
    end_send,
    row_recv,
    got_near_recv,
    got_far_recv,
    group_sem,
):
    blocks, rows, width = own.shape
    quarter = rows // REP
    piece = quarter // PIECES
    count = blocks * PIECES
    place = lax.axis_index("blk")
    y = lax.axis_index("rep")
    core = lax.rem(place, 2)
    first = core == 0

    def phys(o):
        return jnp.where(first, o, blocks - 1 - o)

    def within(distance):
        return jnp.logical_and(place + distance >= 0, place + distance < places)

    sibling = place + 1 - 2 * core
    forth = jnp.where(first, -2, 2)
    sends_to = place + forth
    gets_from = place - forth
    sends, gets = within(forth), within(-forth)
    gets_near = within(1)

    def piece_rows(i):
        return pl.ds(pl.multiple_of(y * quarter + (i % PIECES) * piece, piece), piece)

    loads = []
    for i in range(count):
        o = i // PIECES
        loads.append(
            pltpu.make_async_copy(
                emb.at[phys(o), piece_rows(i), :],
                stage.at[o, piece_rows(i), :],
                load_sem.at[i],
            )
        )
    rest = []
    for j in range(1, REP):
        span = pl.ds(pl.multiple_of(lax.rem(y + j, REP) * quarter, quarter), quarter)
        for o in range(blocks):
            rest.append((o, span))
            loads.append(
                pltpu.make_async_copy(
                    emb.at[phys(o), span, :],
                    stage.at[o, span, :],
                    load_sem.at[count + len(rest) - 1],
                )
            )
    pairs_load = pltpu.make_async_copy(pairs, pairs_there, pair_sem.at[0])
    pairs_load.start()
    for load in loads:
        load.start()
    pairs_load_s = pltpu.make_async_copy(pairs, pairs_here, pair_sem.at[1])
    pairs_load_s.start()

    row_max[...] = jnp.full(row_max.shape, -1.0, jnp.float32)
    msg_row[...] = jnp.full(msg_row.shape, -1.0, jnp.float32)
    got_near[...] = jnp.full(got_near.shape, -1.0, jnp.float32)
    got_far[...] = jnp.full(got_far.shape, -1.0, jnp.float32)
    pairs_far[...] = jnp.zeros(pairs_far.shape, jnp.int32)

    barrier = pltpu.get_barrier_semaphore()
    around = (-2, -1, 1, 2)
    for d in around:

        @pl.when(within(d))
        def _():
            pl.semaphore_signal(
                barrier, inc=1, device_id={"blk": place + d}, device_id_type=MESH
            )

    for j in range(1, REP):
        pl.semaphore_signal(
            barrier, inc=1, device_id={"rep": lax.rem(y + j, REP)}, device_id_type=MESH
        )
    neighbours = sum(within(d).astype(jnp.int32) for d in around)
    pl.semaphore_wait(barrier, neighbours + REP - 1)
    for d in around:

        @pl.when(within(d))
        def _():
            pl.semaphore_signal(
                group_sem, inc=1, device_id={"blk": place + d}, device_id_type=MESH
            )

    def unit(block):
        squares = jnp.sum(block * block, axis=1, keepdims=True)
        return (block * lax.rsqrt(squares + 1e-06)).astype(jnp.bfloat16)

    def part(i):
        return pl.ds((i % PIECES) * piece, piece)

    def far_copy(i):
        return pltpu.make_async_remote_copy(
            src_ref=mine.at[i // PIECES, part(i), :],
            dst_ref=far.at[i // PIECES, part(i), :],
            send_sem=far_send.at[i],
            recv_sem=far_recv.at[i],
            device_id={"blk": sends_to},
            device_id_type=MESH,
        )

    def near_copy(i, source):
        return pltpu.make_async_remote_copy(
            src_ref=source.at[i // PIECES, part(i), :],
            dst_ref=near.at[i // PIECES, part(i), :],
            send_sem=near_send.at[i],
            recv_sem=near_recv.at[i],
            device_id={"blk": sibling},
            device_id_type=MESH,
        )

    pairs_load.wait()
    pairs_copy = pltpu.make_async_remote_copy(
        src_ref=pairs_there,
        dst_ref=pairs_far,
        send_sem=pair_sem.at[2],
        recv_sem=pair_sem.at[3],
        device_id={"blk": place + 2},
        device_id_type=MESH,
    )

    @pl.when(within(2))
    def _():
        pairs_copy.start()

    for i in range(count):
        o = i // PIECES
        loads[i].wait()
        value = unit(stage[o, piece_rows(i), :])
        mine[o, part(i), :] = value
        own[o, piece_rows(i), :] = value

        @pl.when(sends)
        def _():
            far_copy(i).start()

        @pl.when(core == 1)
        def _():
            near_copy(i, mine).start()

    for n, (o, span) in enumerate(rest):
        loads[count + n].wait()
        own[o, span, :] = unit(stage[o, span, :])

    @pl.when(within(-2))
    def _():
        pairs_copy.wait_recv()

    pairs_move = pltpu.make_async_copy(pairs_far, pairs_far_s, pair_sem.at[4])
    pairs_move.start()
    pairs_load_s.wait()
    pairs_move.wait()

    def cap(listed):
        return listed.astype(jnp.float32) * 1e30 - 1.0

    def own_cap(o1, o2):
        return cap(pairs_here[jnp.where(first, o1, blocks - 1 - o2), o2 - o1 - 1])

    def near_cap(o, q):
        return cap(
            pairs_here[
                jnp.where(first, o, blocks - 1 - o),
                jnp.where(first, 2 * blocks - 2 - q - o, o + q),
            ]
        )

    def far_cap(o, q):
        here = pairs_here[o, 2 * blocks - 1 + q - o]
        there = pairs_far_s[blocks - 1 - q, 2 * blocks - 1 + q - o]
        return cap(jnp.where(first, here, there))

    def multiply(left, targets):
        kept = None
        for o, limit in targets:
            mine_max = None
            for c in range(rows // LANES):
                lanes = pl.ds(c * LANES, LANES)
                sim = lax.dot_general(
                    left, own[o, lanes, :], NT, preferred_element_type=jnp.float32
                )
                down = jnp.minimum(fold_rows(sim), limit)
                row_max[o, :, lanes] = jnp.maximum(row_max[o, :, lanes], down)
                across = fold_lanes(sim)
                mine_max = across if mine_max is None else jnp.maximum(mine_max, across)
            mine_max = jnp.minimum(mine_max, limit)
            kept = mine_max if kept is None else jnp.maximum(kept, mine_max)
        turned = [
            jnp.max(kept[128 * j : 128 * (j + 1), :].T, axis=0, keepdims=True)
            for j in range(quarter // 128)
        ]
        return jnp.concatenate(turned, axis=1)

    lanes_here = pl.ds(pl.multiple_of(y * quarter, quarter), quarter)
    for q in range(blocks - 1):
        targets = [(o, own_cap(q, o)) for o in range(q + 1, blocks)]
        msg_row[q, :, lanes_here] = multiply(mine[q], targets)

    def near_tiles(q):
        targets = [(o, near_cap(o, q)) for o in range(blocks)]
        msg_near[q] = multiply(near[q], targets)

    def far_tiles(q):
        targets = [(o, far_cap(o, q)) for o in range(q, blocks)]
        msg_far[q] = multiply(far[q], targets)

    def relay(i):
        far_copy(i).wait_recv()
        near_copy(i, far).start()

    half = PIECES // 2
    for q in range(blocks):
        pieces = range(q * PIECES, (q + 1) * PIECES)

        @pl.when(core == 0)
        def _():
            @pl.when(gets)
            def _():
                for i in pieces[:half]:
                    relay(i)

            for i in pieces:
                near_copy(i, mine).wait_recv()
            near_tiles(q)

            @pl.when(gets)
            def _():
                for i in pieces[half:]:
                    relay(i)
                far_tiles(q)

        @pl.when(core == 1)
        def _():
            @pl.when(gets)
            def _():
                for i in pieces:
                    far_copy(i).wait_recv()
                far_tiles(q)

            @pl.when(gets_near)
            def _():
                for i in pieces:
                    near_copy(i, mine).wait_recv()
                near_tiles(q)

    for o in range(blocks):
        msg_row[o] = jnp.maximum(msg_row[o], jnp.max(row_max[o], axis=0, keepdims=True))

    def end_copy(k, source, target, recv, blk, rep):
        return pltpu.make_async_remote_copy(
            src_ref=source,
            dst_ref=target.at[y],
            send_sem=end_send.at[k],
            recv_sem=recv.at[y],
            device_id={"blk": blk, "rep": rep},
            device_id_type=MESH,
        )

    near_ends, far_ends, row_ends = [], [], []
    for j in range(REP):
        rep = lax.rem(y + j, REP)
        near_ends.append(
            end_copy(3 * j, msg_near, got_near, got_near_recv, place + 1, rep)
        )
        far_ends.append(
            end_copy(3 * j + 1, msg_far, got_far, got_far_recv, gets_from, rep)
        )
        if j:
            row_ends.append(
                end_copy(3 * j + 2, msg_row, got_row, row_recv, place, rep)
            )
    ends = ((gets_near, near_ends), (gets, far_ends), (None, row_ends))

    def each(act):
        for condition, copies in ends:
            if condition is None:
                for copy in copies:
                    act(copy)
            else:

                @pl.when(condition)
                def _():
                    for copy in copies:
                        act(copy)

    pl.semaphore_wait(group_sem, neighbours)
    each(lambda copy: copy.start())

    def arrived(source, target, recv, slot):
        pltpu.make_async_remote_copy(
            src_ref=source,
            dst_ref=target.at[slot],
            send_sem=end_send.at[0],
            recv_sem=recv.at[slot],
            device_id={"rep": lax.rem(y + 1, REP)},
            device_id_type=MESH,
        ).wait_recv()

    for j in range(REP):
        slot = lax.rem(y + j, REP)

        @pl.when(within(-1))
        def _():
            arrived(msg_near, got_near, got_near_recv, slot)

        @pl.when(sends)
        def _():
            arrived(msg_far, got_far, got_far_recv, slot)

        if j:
            arrived(msg_row, got_row, row_recv, slot)

    best = []
    for o in range(blocks):
        value = msg_row[o]
        for j in range(1, REP):
            value = jnp.maximum(value, got_row[lax.rem(y + j, REP), o])
        side = [jnp.maximum(got_near[j, o], got_far[j, o]) for j in range(REP)]
        best.append(jnp.maximum(value, jnp.concatenate(side, axis=1)))
    for o in range(blocks):
        out[o : o + 1, :] = jnp.where(first, best[o], best[blocks - 1 - o])

    each(lambda copy: copy.wait_send())

    @pl.when(within(2))
    def _():
        pairs_copy.wait_send()

    @pl.when(sends)
    def _():
        for i in range(count):
            far_copy(i).wait_send()

    @pl.when(jnp.logical_or(core == 1, gets))
    def _():
        for i in range(count):
            near_copy(i, mine).wait_send()


def solution(mesh):
    places = mesh.shape["blk"]

    def per_device(embeddings, pairs):
        blocks, rows, width = embeddings.shape
        reach = pairs.shape[1]
        quarter = rows // REP
        count = blocks * PIECES
        dma = pltpu.SemaphoreType.DMA

        def body(*refs):
            kernel(places, *refs)

        return pl.pallas_call(
            body,
            out_shape=jax.ShapeDtypeStruct((blocks, rows), jnp.float32),
            in_specs=[pl.BlockSpec(memory_space=pltpu.HBM)] * 2,
            out_specs=pl.BlockSpec(memory_space=pltpu.VMEM),
            scratch_shapes=[
                pltpu.VMEM((blocks, rows, width), jnp.float32),
                pltpu.VMEM((blocks, rows, width), jnp.bfloat16),
                pltpu.VMEM((blocks, quarter, width), jnp.bfloat16),
                pltpu.VMEM((blocks, quarter, width), jnp.bfloat16),
                pltpu.VMEM((blocks, quarter, width), jnp.bfloat16),
                pltpu.VMEM((blocks, 8, rows), jnp.float32),
                pltpu.SMEM((blocks, reach), jnp.int32),
                pltpu.VMEM((blocks, reach), jnp.int32),
                pltpu.VMEM((blocks, reach), jnp.int32),
                pltpu.SMEM((blocks, reach), jnp.int32),
                pltpu.VMEM((blocks, 1, rows), jnp.float32),
                pltpu.VMEM((blocks, 1, quarter), jnp.float32),
                pltpu.VMEM((blocks, 1, quarter), jnp.float32),
                pltpu.VMEM((REP, blocks, 1, rows), jnp.float32),
                pltpu.VMEM((REP, blocks, 1, quarter), jnp.float32),
                pltpu.VMEM((REP, blocks, 1, quarter), jnp.float32),
                dma((count + (REP - 1) * blocks,)),
                dma((5,)),
                dma((count,)),
                dma((count,)),
                dma((count,)),
                dma((count,)),
                dma((3 * REP,)),
                dma((REP,)),
                dma((REP,)),
                dma((REP,)),
                pltpu.SemaphoreType.REGULAR,
            ],
            compiler_params=pltpu.CompilerParams(
                collective_id=0, has_side_effects=True, vmem_limit_bytes=56 << 20
            ),
            name="neighbours",
        )(embeddings, pairs)

    return jax.shard_map(
        per_device,
        mesh=mesh,
        in_specs=(P("blk", None, None), P("blk", None)),
        out_specs=P("blk", None),
        check_vma=False,
    )
```

```python
import jax
import jax.numpy as jnp
from jax import lax
from jax.experimental import pallas as pl
from jax.experimental.pallas import tpu as pltpu
from jax.sharding import PartitionSpec as P

MESH = pl.DeviceIdType.MESH
REP = 4
PIECES = 4
LANES = 256
NT = (((1,), (1,)), ((), ()))


def fold_lanes(sim):
    out = sim[:, :128]
    for j in range(1, sim.shape[1] // 128):
        out = jnp.maximum(out, sim[:, 128 * j : 128 * (j + 1)])
    return out


def fold_rows(sim):
    return jnp.max(sim.reshape(-1, 8, sim.shape[1]), axis=0)


def kernel(
    places,
    emb,
    pairs,
    out,
    stage,
    own,
    mine,
    near,
    far,
    row_max,
    pairs_here,
    pairs_there,
    pairs_far,
    pairs_far_s,
    msg_row,
    msg_near,
    msg_far,
    got_row,
    got_near,
    got_far,
    load_sem,
    pair_sem,
    far_send,
    far_recv,
    near_send,
    near_recv,
    relay_send,
    end_send,
    row_recv,
    got_near_recv,
    got_far_recv,
    group_sem,
):
    blocks, rows, width = own.shape
    quarter = rows // REP
    piece = quarter // PIECES
    count = blocks * PIECES
    place = lax.axis_index("blk")
    y = lax.axis_index("rep")
    core = lax.rem(place, 2)
    first = core == 0

    def phys(o):
        return jnp.where(first, o, blocks - 1 - o)

    def within(distance):
        return jnp.logical_and(place + distance >= 0, place + distance < places)

    sibling = place + 1 - 2 * core
    forth = jnp.where(first, -2, 2)
    sends_to = place + forth
    gets_from = place - forth
    sends, gets = within(forth), within(-forth)
    gets_near = within(1)

    got_near[...] = jnp.full(got_near.shape, -1.0, jnp.float32)
    got_far[...] = jnp.full(got_far.shape, -1.0, jnp.float32)
    pairs_far[...] = jnp.zeros(pairs_far.shape, jnp.int32)

    barrier = pltpu.get_barrier_semaphore()
    around = (-2, -1, 1, 2)
    for d in around:

        @pl.when(within(d))
        def _():
            pl.semaphore_signal(
                barrier, inc=1, device_id={"blk": place + d}, device_id_type=MESH
            )

    for j in range(1, REP):
        pl.semaphore_signal(
            barrier, inc=1, device_id={"rep": lax.rem(y + j, REP)}, device_id_type=MESH
        )
    def piece_rows(i):
        return pl.ds(pl.multiple_of(y * quarter + (i % PIECES) * piece, piece), piece)

    loads = []
    for i in range(count):
        o = i // PIECES
        loads.append(
            pltpu.make_async_copy(
                emb.at[phys(o), piece_rows(i), :],
                stage.at[o, piece_rows(i), :],
                load_sem.at[i],
            )
        )
    rest = []
    for j in range(1, REP):
        span = pl.ds(pl.multiple_of(lax.rem(y + j, REP) * quarter, quarter), quarter)
        for o in range(blocks):
            rest.append((o, span))
            loads.append(
                pltpu.make_async_copy(
                    emb.at[phys(o), span, :],
                    stage.at[o, span, :],
                    load_sem.at[count + len(rest) - 1],
                )
            )
    pairs_load = pltpu.make_async_copy(pairs, pairs_there, pair_sem.at[0])
    pairs_load.start()
    for load in loads[:count]:
        load.start()
    pairs_load_s = pltpu.make_async_copy(pairs, pairs_here, pair_sem.at[1])
    pairs_load_s.start()

    row_max[...] = jnp.full(row_max.shape, -1.0, jnp.float32)
    msg_row[...] = jnp.full(msg_row.shape, -1.0, jnp.float32)

    neighbours = sum(within(d).astype(jnp.int32) for d in around)
    def unit(block):
        squares = jnp.sum(block * block, axis=1, keepdims=True)
        return (block * lax.rsqrt(squares + 1e-06)).astype(jnp.bfloat16)

    def part(i):
        return pl.ds((i % PIECES) * piece, piece)

    def far_copy(i):
        return pltpu.make_async_remote_copy(
            src_ref=mine.at[i // PIECES, part(i), :],
            dst_ref=far.at[i // PIECES, part(i), :],
            send_sem=far_send.at[i],
            recv_sem=far_recv.at[i],
            device_id={"blk": sends_to},
            device_id_type=MESH,
        )

    def last_copy(i):
        return pltpu.make_async_remote_copy(
            src_ref=mine.at[i // PIECES, part(i), :],
            dst_ref=near.at[i // PIECES, part(i), :],
            send_sem=far_send.at[i],
            recv_sem=near_recv.at[i],
            device_id={"blk": place - 1},
            device_id_type=MESH,
        )

    def to_sibling(i, source, target, send, recv):
        return pltpu.make_async_remote_copy(
            src_ref=source.at[i // PIECES, part(i), :],
            dst_ref=target.at[i // PIECES, part(i), :],
            send_sem=send.at[i],
            recv_sem=recv.at[i],
            device_id={"blk": sibling},
            device_id_type=MESH,
        )

    def near_copy(i):
        return to_sibling(i, mine, near, near_send, near_recv)

    def relay_copy(i):
        if i < last:
            return to_sibling(i, far, near, relay_send, near_recv)
        return to_sibling(i, near, far, relay_send, far_recv)

    pairs_copy = pltpu.make_async_remote_copy(
        src_ref=pairs_there,
        dst_ref=pairs_far,
        send_sem=pair_sem.at[2],
        recv_sem=pair_sem.at[3],
        device_id={"blk": place + 2},
        device_id_type=MESH,
    )
    last = count - PIECES
    for i in range(count):
        o = i // PIECES
        loads[i].wait()
        if i == 1:
            for load in loads[count:]:
                load.start()
        value = unit(stage[o, piece_rows(i), :])
        mine[o, part(i), :] = value
        own[o, piece_rows(i), :] = value
        if i == 0:
            pairs_load.wait()
            pl.semaphore_wait(barrier, neighbours + REP - 1)

            @pl.when(within(2))
            def _():
                pairs_copy.start()

        if i < last:

            @pl.when(sends)
            def _():
                far_copy(i).start()

        else:

            @pl.when(jnp.logical_and(core == 0, sends))
            def _():
                last_copy(i).start()

            @pl.when(jnp.logical_and(core == 1, sends))
            def _():
                far_copy(i).start()

        @pl.when(core == 1)
        def _():
            near_copy(i).start()

    for d in around:

        @pl.when(within(d))
        def _():
            pl.semaphore_signal(
                group_sem, inc=1, device_id={"blk": place + d}, device_id_type=MESH
            )

    for n, (o, span) in enumerate(rest):
        loads[count + n].wait()
        own[o, span, :] = unit(stage[o, span, :])

    @pl.when(within(-2))
    def _():
        pairs_copy.wait_recv()

    pairs_move = pltpu.make_async_copy(pairs_far, pairs_far_s, pair_sem.at[4])
    pairs_move.start()
    pairs_load_s.wait()
    pairs_move.wait()

    def cap(listed):
        return listed.astype(jnp.float32) * 1e30 - 1.0

    def own_cap(o1, o2):
        return cap(pairs_here[jnp.where(first, o1, blocks - 1 - o2), o2 - o1 - 1])

    def near_cap(o, q):
        return cap(
            pairs_here[
                jnp.where(first, o, blocks - 1 - o),
                jnp.where(first, 2 * blocks - 2 - q - o, o + q),
            ]
        )

    def far_cap(o, q):
        here = pairs_here[o, 2 * blocks - 1 + q - o]
        there = pairs_far_s[blocks - 1 - q, 2 * blocks - 1 + q - o]
        return cap(jnp.where(first, here, there))

    def multiply(left, targets):
        kept = None
        for o, limit in targets:
            mine_max = None
            for c in range(rows // LANES):
                lanes = pl.ds(c * LANES, LANES)
                sim = lax.dot_general(
                    left, own[o, lanes, :], NT, preferred_element_type=jnp.float32
                )
                down = jnp.minimum(fold_rows(sim), limit)
                row_max[o, :, lanes] = jnp.maximum(row_max[o, :, lanes], down)
                across = fold_lanes(sim)
                mine_max = across if mine_max is None else jnp.maximum(mine_max, across)
            mine_max = jnp.minimum(mine_max, limit)
            kept = mine_max if kept is None else jnp.maximum(kept, mine_max)
        turned = [
            jnp.max(kept[128 * j : 128 * (j + 1), :].T, axis=0, keepdims=True)
            for j in range(quarter // 128)
        ]
        return jnp.concatenate(turned, axis=1)

    lanes_here = pl.ds(pl.multiple_of(y * quarter, quarter), quarter)
    for q in range(blocks - 1):
        targets = [(o, own_cap(q, o)) for o in range(q + 1, blocks)]
        msg_row[q, :, lanes_here] = multiply(mine[q], targets)

    def near_tiles(q):
        targets = [(o, near_cap(o, q)) for o in range(blocks)]
        msg_near[q] = multiply(near[q], targets)

    def far_tiles(q):
        targets = [(o, far_cap(o, q)) for o in range(q, blocks)]
        msg_far[q] = multiply(far[q], targets)

    def end_copy(k, source, target, recv, blk, rep):
        return pltpu.make_async_remote_copy(
            src_ref=source,
            dst_ref=target.at[y],
            send_sem=end_send.at[k],
            recv_sem=recv.at[y],
            device_id={"blk": blk, "rep": rep},
            device_id_type=MESH,
        )

    near_ends, far_ends, row_ends = [], [], []
    for j in range(REP):
        rep = lax.rem(y + REP - j, REP)
        near_ends.append(
            end_copy(3 * j, msg_near, got_near, got_near_recv, place + 1, rep)
        )
        far_ends.append(
            end_copy(3 * j + 1, msg_far, got_far, got_far_recv, gets_from, rep)
        )
        if j:
            row_ends.append(
                end_copy(3 * j + 2, msg_row, got_row, row_recv, place, rep)
            )

    def fold(o):
        msg_row[o] = jnp.maximum(
            msg_row[o], jnp.max(row_max[o], axis=0, keepdims=True)
        )

    def relay(i):
        (far_copy(i) if i < last else near_copy(i)).wait_recv()
        relay_copy(i).start()

    half = PIECES // 2
    for q in range(blocks - 1):
        pieces = range(q * PIECES, (q + 1) * PIECES)

        @pl.when(core == 0)
        def _():
            @pl.when(gets)
            def _():
                for i in pieces[:half]:
                    relay(i)

            for i in pieces:
                near_copy(i).wait_recv()
            near_tiles(q)

            @pl.when(gets)
            def _():
                for i in pieces[half:]:
                    relay(i)
                far_tiles(q)

        @pl.when(core == 1)
        def _():
            @pl.when(gets)
            def _():
                for i in pieces:
                    far_copy(i).wait_recv()
                far_tiles(q)

            @pl.when(gets_near)
            def _():
                for i in pieces:
                    near_copy(i).wait_recv()
                near_tiles(q)

    pl.semaphore_wait(group_sem, neighbours)

    @pl.when(gets_near)
    def _():
        @pl.when(core == 0)
        def _():
            for i in range(last, count):
                near_copy(i).wait_recv()

        @pl.when(core == 1)
        def _():
            for i in range(last, count):
                relay(i)

        near_tiles(blocks - 1)
        for copy in near_ends:
            copy.start()

    for o in range(blocks - 1):
        fold(o)

    @pl.when(gets)
    def _():
        for i in range(last, count):
            far_copy(i).wait_recv()
        far_tiles(blocks - 1)
        for copy in far_ends:
            copy.start()

    fold(blocks - 1)
    for copy in row_ends:
        copy.start()

    def arrived(source, target, recv, slot):
        pltpu.make_async_remote_copy(
            src_ref=source,
            dst_ref=target.at[slot],
            send_sem=end_send.at[0],
            recv_sem=recv.at[slot],
            device_id={"rep": lax.rem(y + 1, REP)},
            device_id_type=MESH,
        ).wait_recv()

    @pl.when(within(-1))
    def _():
        for j in range(REP):
            arrived(msg_near, got_near, got_near_recv, lax.rem(y + j, REP))

    @pl.when(sends)
    def _():
        for j in range(REP):
            arrived(msg_far, got_far, got_far_recv, lax.rem(y + j, REP))

    for j in range(1, REP):
        arrived(msg_row, got_row, row_recv, lax.rem(y + j, REP))

    best = []
    for o in range(blocks):
        value = msg_row[o]
        for j in range(1, REP):
            value = jnp.maximum(value, got_row[lax.rem(y + j, REP), o])
        side = [jnp.maximum(got_near[j, o], got_far[j, o]) for j in range(REP)]
        best.append(jnp.maximum(value, jnp.concatenate(side, axis=1)))
    for o in range(blocks):
        out[o : o + 1, :] = jnp.where(first, best[o], best[blocks - 1 - o])

    for copy in row_ends:
        copy.wait_send()

    @pl.when(gets_near)
    def _():
        for copy in near_ends:
            copy.wait_send()

    @pl.when(gets)
    def _():
        for copy in far_ends:
            copy.wait_send()

    @pl.when(within(2))
    def _():
        pairs_copy.wait_send()

    @pl.when(sends)
    def _():
        for i in range(count):
            far_copy(i).wait_send()

    @pl.when(core == 1)
    def _():
        for i in range(count):
            near_copy(i).wait_send()

        @pl.when(gets_near)
        def _():
            for i in range(last, count):
                relay_copy(i).wait_send()

    @pl.when(jnp.logical_and(core == 0, gets))
    def _():
        for i in range(last):
            relay_copy(i).wait_send()


def solution(mesh):
    places = mesh.shape["blk"]

    def per_device(embeddings, pairs):
        blocks, rows, width = embeddings.shape
        reach = pairs.shape[1]
        quarter = rows // REP
        count = blocks * PIECES
        dma = pltpu.SemaphoreType.DMA

        def body(*refs):
            kernel(places, *refs)

        return pl.pallas_call(
            body,
            out_shape=jax.ShapeDtypeStruct((blocks, rows), jnp.float32),
            in_specs=[pl.BlockSpec(memory_space=pltpu.HBM)] * 2,
            out_specs=pl.BlockSpec(memory_space=pltpu.VMEM),
            scratch_shapes=[
                pltpu.VMEM((blocks, rows, width), jnp.float32),
                pltpu.VMEM((blocks, rows, width), jnp.bfloat16),
                pltpu.VMEM((blocks, quarter, width), jnp.bfloat16),
                pltpu.VMEM((blocks, quarter, width), jnp.bfloat16),
                pltpu.VMEM((blocks, quarter, width), jnp.bfloat16),
                pltpu.VMEM((blocks, 8, rows), jnp.float32),
                pltpu.SMEM((blocks, reach), jnp.int32),
                pltpu.VMEM((blocks, reach), jnp.int32),
                pltpu.VMEM((blocks, reach), jnp.int32),
                pltpu.SMEM((blocks, reach), jnp.int32),
                pltpu.VMEM((blocks, 1, rows), jnp.float32),
                pltpu.VMEM((blocks, 1, quarter), jnp.float32),
                pltpu.VMEM((blocks, 1, quarter), jnp.float32),
                pltpu.VMEM((REP, blocks, 1, rows), jnp.float32),
                pltpu.VMEM((REP, blocks, 1, quarter), jnp.float32),
                pltpu.VMEM((REP, blocks, 1, quarter), jnp.float32),
                dma((count + (REP - 1) * blocks,)),
                dma((5,)),
                dma((count,)),
                dma((count,)),
                dma((count,)),
                dma((count,)),
                dma((count,)),
                dma((3 * REP,)),
                dma((REP,)),
                dma((REP,)),
                dma((REP,)),
                pltpu.SemaphoreType.REGULAR,
            ],
            compiler_params=pltpu.CompilerParams(
                collective_id=0, has_side_effects=True, vmem_limit_bytes=56 << 20
            ),
            name="neighbours",
        )(embeddings, pairs)

    return jax.shard_map(
        per_device,
        mesh=mesh,
        in_specs=(P("blk", None, None), P("blk", None)),
        out_specs=P("blk", None),
        check_vma=False,
    )
```

```python
import jax
import jax.numpy as jnp
from jax import lax
from jax.experimental import pallas as pl
from jax.experimental.pallas import tpu as pltpu
from jax.sharding import PartitionSpec as P

MESH = pl.DeviceIdType.MESH
REP = 4
CUTS = ((2, 2), (2, 2), (2, 4, 4))
LANES = 256
NT = (((1,), (1,)), ((), ()))


def fold_lanes(sim):
    out = sim[:, :128]
    for j in range(1, sim.shape[1] // 128):
        out = jnp.maximum(out, sim[:, 128 * j : 128 * (j + 1)])
    return out


def fold_rows(sim):
    return jnp.max(sim.reshape(-1, 8, sim.shape[1]), axis=0)


def kernel(
    places,
    emb,
    pairs,
    out,
    stage,
    own,
    mine,
    near,
    far,
    row_max,
    pairs_here,
    pairs_there,
    pairs_far,
    pairs_far_s,
    msg_row,
    msg_near,
    msg_far,
    got_row,
    got_near,
    got_far,
    load_sem,
    pair_sem,
    far_send,
    far_recv,
    near_send,
    near_recv,
    relay_send,
    end_send,
    row_recv,
    got_near_recv,
    got_far_recv,
    group_sem,
):
    blocks, rows, width = own.shape
    quarter = rows // REP
    parts = []
    for o, cut in enumerate(CUTS):
        start = 0
        for share in cut:
            parts.append((o, start, quarter // share))
            start += quarter // share
    count = len(parts)
    place = lax.axis_index("blk")
    y = lax.axis_index("rep")
    core = lax.rem(place, 2)
    first = core == 0

    def phys(o):
        return jnp.where(first, o, blocks - 1 - o)

    def within(distance):
        return jnp.logical_and(place + distance >= 0, place + distance < places)

    sibling = place + 1 - 2 * core
    forth = jnp.where(first, -2, 2)
    sends_to = place + forth
    gets_from = place - forth
    sends, gets = within(forth), within(-forth)
    gets_near = within(1)

    barrier = pltpu.get_barrier_semaphore()
    around = (-forth, forth, 1, -1)
    for d in around:

        @pl.when(within(d))
        def _():
            pl.semaphore_signal(
                barrier, inc=1, device_id={"blk": place + d}, device_id_type=MESH
            )

    for j in (2, 1, 3):
        pl.semaphore_signal(
            barrier, inc=1, device_id={"rep": lax.rem(y + j, REP)}, device_id_type=MESH
        )

    def piece_rows(i):
        _, start, size = parts[i]
        return pl.ds(pl.multiple_of(y * quarter + start, size), size)

    loads = []
    for i in range(count):
        o = parts[i][0]
        loads.append(
            pltpu.make_async_copy(
                emb.at[phys(o), piece_rows(i), :],
                stage.at[o, piece_rows(i), :],
                load_sem.at[i],
            )
        )
    rest = []
    for j in range(1, REP):
        span = pl.ds(pl.multiple_of(lax.rem(y + j, REP) * quarter, quarter), quarter)
        for o in range(blocks):
            rest.append((o, span))
            loads.append(
                pltpu.make_async_copy(
                    emb.at[phys(o), span, :],
                    stage.at[o, span, :],
                    load_sem.at[count + len(rest) - 1],
                )
            )
    pairs_load = pltpu.make_async_copy(pairs, pairs_there, pair_sem.at[0])
    pairs_load.start()
    for load in loads[:count]:
        load.start()
    pairs_load_s = pltpu.make_async_copy(pairs, pairs_here, pair_sem.at[1])
    pairs_load_s.start()

    row_max[...] = jnp.full(row_max.shape, -1.0, jnp.float32)
    msg_row[...] = jnp.full(msg_row.shape, -1.0, jnp.float32)


    @pl.when(jnp.logical_not(within(-1)))
    def _():
        got_near[...] = jnp.full(got_near.shape, -1.0, jnp.float32)

    @pl.when(jnp.logical_not(sends))
    def _():
        got_far[...] = jnp.full(got_far.shape, -1.0, jnp.float32)

    @pl.when(jnp.logical_not(within(-2)))
    def _():
        pairs_far[...] = jnp.zeros(pairs_far.shape, jnp.int32)

    neighbours = sum(within(d).astype(jnp.int32) for d in around)
    def unit(block):
        squares = jnp.sum(block * block, axis=1, keepdims=True)
        return (block * lax.rsqrt(squares + 1e-06)).astype(jnp.bfloat16)

    def part(i):
        _, start, size = parts[i]
        return pl.ds(start, size)

    def of_block(q):
        return [i for i in range(count) if parts[i][0] == q]

    def far_copy(i):
        return pltpu.make_async_remote_copy(
            src_ref=mine.at[parts[i][0], part(i), :],
            dst_ref=far.at[parts[i][0], part(i), :],
            send_sem=far_send.at[i],
            recv_sem=far_recv.at[i],
            device_id={"blk": sends_to},
            device_id_type=MESH,
        )

    def last_copy(i):
        return pltpu.make_async_remote_copy(
            src_ref=mine.at[parts[i][0], part(i), :],
            dst_ref=near.at[parts[i][0], part(i), :],
            send_sem=far_send.at[i],
            recv_sem=near_recv.at[i],
            device_id={"blk": place - 1},
            device_id_type=MESH,
        )

    def to_sibling(i, source, target, send, recv):
        return pltpu.make_async_remote_copy(
            src_ref=source.at[parts[i][0], part(i), :],
            dst_ref=target.at[parts[i][0], part(i), :],
            send_sem=send.at[i],
            recv_sem=recv.at[i],
            device_id={"blk": sibling},
            device_id_type=MESH,
        )

    def near_copy(i):
        return to_sibling(i, mine, near, near_send, near_recv)

    def relay_copy(i):
        if i < last:
            return to_sibling(i, far, near, relay_send, near_recv)
        return to_sibling(i, near, far, relay_send, far_recv)

    pairs_copy = pltpu.make_async_remote_copy(
        src_ref=pairs_there,
        dst_ref=pairs_far,
        send_sem=pair_sem.at[2],
        recv_sem=pair_sem.at[3],
        device_id={"blk": place + 2},
        device_id_type=MESH,
    )
    last = of_block(blocks - 1)[0]
    for i in range(count):
        o = parts[i][0]
        loads[i].wait()
        if i == 1:
            for load in loads[count:]:
                load.start()
        value = unit(stage[o, piece_rows(i), :])
        mine[o, part(i), :] = value
        own[o, piece_rows(i), :] = value
        if i == 0:
            pairs_load.wait()
            pl.semaphore_wait(barrier, neighbours + REP - 1)

            @pl.when(within(2))
            def _():
                pairs_copy.start()

        if i < last:

            @pl.when(sends)
            def _():
                far_copy(i).start()

        else:

            @pl.when(jnp.logical_and(core == 0, sends))
            def _():
                last_copy(i).start()

            @pl.when(jnp.logical_and(core == 1, sends))
            def _():
                far_copy(i).start()

        @pl.when(core == 1)
        def _():
            near_copy(i).start()

    for d in around:

        @pl.when(within(d))
        def _():
            pl.semaphore_signal(
                group_sem, inc=1, device_id={"blk": place + d}, device_id_type=MESH
            )

    for n, (o, span) in enumerate(rest):
        loads[count + n].wait()
        own[o, span, :] = unit(stage[o, span, :])

    @pl.when(within(-2))
    def _():
        pairs_copy.wait_recv()

    pairs_move = pltpu.make_async_copy(pairs_far, pairs_far_s, pair_sem.at[4])
    pairs_move.start()
    pairs_load_s.wait()
    pairs_move.wait()

    def cap(listed):
        return listed.astype(jnp.float32) * 1e30 - 1.0

    def own_cap(o1, o2):
        return cap(pairs_here[jnp.where(first, o1, blocks - 1 - o2), o2 - o1 - 1])

    def near_cap(o, q):
        return cap(
            pairs_here[
                jnp.where(first, o, blocks - 1 - o),
                jnp.where(first, 2 * blocks - 2 - q - o, o + q),
            ]
        )

    def far_cap(o, q):
        here = pairs_here[o, 2 * blocks - 1 + q - o]
        there = pairs_far_s[blocks - 1 - q, 2 * blocks - 1 + q - o]
        return cap(jnp.where(first, here, there))

    def multiply(left, targets):
        kept = None
        for o, limit in targets:
            mine_max = None
            for c in range(rows // LANES):
                lanes = pl.ds(c * LANES, LANES)
                sim = lax.dot_general(
                    left, own[o, lanes, :], NT, preferred_element_type=jnp.float32
                )
                down = jnp.minimum(fold_rows(sim), limit)
                row_max[o, :, lanes] = jnp.maximum(row_max[o, :, lanes], down)
                across = fold_lanes(sim)
                mine_max = across if mine_max is None else jnp.maximum(mine_max, across)
            mine_max = jnp.minimum(mine_max, limit)
            kept = mine_max if kept is None else jnp.maximum(kept, mine_max)
        turned = [
            jnp.max(kept[128 * j : 128 * (j + 1), :].T, axis=0, keepdims=True)
            for j in range(quarter // 128)
        ]
        return jnp.concatenate(turned, axis=1)

    lanes_here = pl.ds(pl.multiple_of(y * quarter, quarter), quarter)
    for q in range(blocks - 1):
        targets = [(o, own_cap(q, o)) for o in range(q + 1, blocks)]
        msg_row[q, :, lanes_here] = multiply(mine[q], targets)

    def near_tiles(q):
        targets = [(o, near_cap(o, q)) for o in range(blocks)]
        msg_near[q] = multiply(near[q], targets)

    def far_tiles(q):
        targets = [(o, far_cap(o, q)) for o in range(q, blocks)]
        msg_far[q] = multiply(far[q], targets)

    def end_copy(k, source, target, recv, blk, rep):
        return pltpu.make_async_remote_copy(
            src_ref=source,
            dst_ref=target.at[y],
            send_sem=end_send.at[k],
            recv_sem=recv.at[y],
            device_id={"blk": blk, "rep": rep},
            device_id_type=MESH,
        )

    near_ends, far_ends, row_ends = [], [], []
    for j in (2, 1, 3, 0):
        rep = lax.rem(y + j, REP)
        near_ends.append(
            end_copy(3 * j, msg_near, got_near, got_near_recv, place + 1, rep)
        )
        far_ends.append(
            end_copy(3 * j + 1, msg_far, got_far, got_far_recv, gets_from, rep)
        )
        if j:
            row_ends.append(
                end_copy(3 * j + 2, msg_row, got_row, row_recv, place, rep)
            )

    def fold(o):
        msg_row[o] = jnp.maximum(
            msg_row[o], jnp.max(row_max[o], axis=0, keepdims=True)
        )

    def relay(i):
        (far_copy(i) if i < last else near_copy(i)).wait_recv()
        relay_copy(i).start()

    for q in range(blocks - 1):
        pieces = of_block(q)
        half = len(pieces) // 2

        @pl.when(core == 0)
        def _():
            @pl.when(gets)
            def _():
                for i in pieces[:half]:
                    relay(i)

            for i in pieces:
                near_copy(i).wait_recv()
            near_tiles(q)

            @pl.when(gets)
            def _():
                for i in pieces[half:]:
                    relay(i)
                far_tiles(q)

        @pl.when(core == 1)
        def _():
            @pl.when(gets)
            def _():
                for i in pieces:
                    far_copy(i).wait_recv()
                far_tiles(q)

            @pl.when(gets_near)
            def _():
                for i in pieces:
                    near_copy(i).wait_recv()
                near_tiles(q)

    pl.semaphore_wait(group_sem, neighbours)

    @pl.when(gets_near)
    def _():
        @pl.when(core == 0)
        def _():
            for i in range(last, count):
                near_copy(i).wait_recv()

        @pl.when(core == 1)
        def _():
            for i in range(last, count):
                relay(i)

        near_tiles(blocks - 1)
        for copy in near_ends:
            copy.start()

    for o in range(blocks - 1):
        fold(o)

    @pl.when(gets)
    def _():
        for i in range(last, count):
            far_copy(i).wait_recv()
        far_tiles(blocks - 1)
        for copy in far_ends:
            copy.start()

    fold(blocks - 1)
    for copy in row_ends:
        copy.start()

    def arrived(source, target, recv, slot):
        pltpu.make_async_remote_copy(
            src_ref=source,
            dst_ref=target.at[slot],
            send_sem=end_send.at[0],
            recv_sem=recv.at[slot],
            device_id={"rep": lax.rem(y + 1, REP)},
            device_id_type=MESH,
        ).wait_recv()

    @pl.when(within(-1))
    def _():
        for j in range(REP):
            arrived(msg_near, got_near, got_near_recv, lax.rem(y + j, REP))

    @pl.when(sends)
    def _():
        for j in range(REP):
            arrived(msg_far, got_far, got_far_recv, lax.rem(y + j, REP))

    for j in range(1, REP):
        arrived(msg_row, got_row, row_recv, lax.rem(y + j, REP))

    best = []
    for o in range(blocks):
        value = msg_row[o]
        for j in range(1, REP):
            value = jnp.maximum(value, got_row[lax.rem(y + j, REP), o])
        side = [jnp.maximum(got_near[j, o], got_far[j, o]) for j in range(REP)]
        best.append(jnp.maximum(value, jnp.concatenate(side, axis=1)))
    for o in range(blocks):
        out[o : o + 1, :] = jnp.where(first, best[o], best[blocks - 1 - o])

    for copy in row_ends:
        copy.wait_send()

    @pl.when(gets_near)
    def _():
        for copy in near_ends:
            copy.wait_send()

    @pl.when(gets)
    def _():
        for copy in far_ends:
            copy.wait_send()

    @pl.when(within(2))
    def _():
        pairs_copy.wait_send()

    @pl.when(sends)
    def _():
        for i in range(count):
            far_copy(i).wait_send()

    @pl.when(core == 1)
    def _():
        for i in range(count):
            near_copy(i).wait_send()

        @pl.when(gets_near)
        def _():
            for i in range(last, count):
                relay_copy(i).wait_send()

    @pl.when(jnp.logical_and(core == 0, gets))
    def _():
        for i in range(last):
            relay_copy(i).wait_send()


def solution(mesh):
    places = mesh.shape["blk"]

    def per_device(embeddings, pairs):
        blocks, rows, width = embeddings.shape
        reach = pairs.shape[1]
        quarter = rows // REP
        count = sum(len(cut) for cut in CUTS)
        dma = pltpu.SemaphoreType.DMA

        def body(*refs):
            kernel(places, *refs)

        return pl.pallas_call(
            body,
            out_shape=pltpu.VMEM((blocks, rows), jnp.float32),
            in_specs=[pl.BlockSpec(memory_space=pltpu.HBM)] * 2,
            out_specs=pl.BlockSpec(memory_space=pltpu.VMEM),
            scratch_shapes=[
                pltpu.VMEM((blocks, rows, width), jnp.float32),
                pltpu.VMEM((blocks, rows, width), jnp.bfloat16),
                pltpu.VMEM((blocks, quarter, width), jnp.bfloat16),
                pltpu.VMEM((blocks, quarter, width), jnp.bfloat16),
                pltpu.VMEM((blocks, quarter, width), jnp.bfloat16),
                pltpu.VMEM((blocks, 8, rows), jnp.float32),
                pltpu.SMEM((blocks, reach), jnp.int32),
                pltpu.VMEM((blocks, reach), jnp.int32),
                pltpu.VMEM((blocks, reach), jnp.int32),
                pltpu.SMEM((blocks, reach), jnp.int32),
                pltpu.VMEM((blocks, 1, rows), jnp.float32),
                pltpu.VMEM((blocks, 1, quarter), jnp.float32),
                pltpu.VMEM((blocks, 1, quarter), jnp.float32),
                pltpu.VMEM((REP, blocks, 1, rows), jnp.float32),
                pltpu.VMEM((REP, blocks, 1, quarter), jnp.float32),
                pltpu.VMEM((REP, blocks, 1, quarter), jnp.float32),
                dma((count + (REP - 1) * blocks,)),
                dma((5,)),
                dma((count,)),
                dma((count,)),
                dma((count,)),
                dma((count,)),
                dma((count,)),
                dma((3 * REP,)),
                dma((REP,)),
                dma((REP,)),
                dma((REP,)),
                pltpu.SemaphoreType.REGULAR,
            ],
            compiler_params=pltpu.CompilerParams(
                collective_id=0, has_side_effects=True, vmem_limit_bytes=56 << 20
            ),
            name="neighbours",
        )(embeddings, pairs)

    return jax.shard_map(
        per_device,
        mesh=mesh,
        in_specs=(P("blk", None, None), P("blk", None)),
        out_specs=P("blk", None),
        check_vma=False,
    )
```

```python
import jax
import jax.numpy as jnp
from jax import lax
from jax.experimental import pallas as pl
from jax.experimental.pallas import tpu as pltpu
from jax.sharding import PartitionSpec as P

MESH = pl.DeviceIdType.MESH
REP = 4
CUTS = ((1,), (1,), (2, 4, 4))
LANES = 256
NT = (((1,), (1,)), ((), ()))


def fold_lanes(sim):
    out = sim[:, :128]
    for j in range(1, sim.shape[1] // 128):
        out = jnp.maximum(out, sim[:, 128 * j : 128 * (j + 1)])
    return out


def fold_rows(sim):
    return jnp.max(sim.reshape(-1, 8, sim.shape[1]), axis=0)


def kernel(
    places,
    emb,
    pairs,
    out,
    stage,
    own,
    mine,
    near,
    far,
    row_max,
    pairs_here,
    pairs_there,
    pairs_far,
    pairs_far_s,
    msg_row,
    msg_near,
    msg_far,
    got_row,
    got_near,
    got_far,
    load_sem,
    pair_sem,
    far_send,
    far_recv,
    near_send,
    near_recv,
    relay_send,
    end_send,
    row_recv,
    got_near_recv,
    got_far_recv,
    group_sem,
):
    blocks, rows, width = own.shape
    quarter = rows // REP
    parts = []
    for o, cut in enumerate(CUTS):
        start = 0
        for share in cut:
            parts.append((o, start, quarter // share))
            start += quarter // share
    count = len(parts)
    place = lax.axis_index("blk")
    y = lax.axis_index("rep")
    core = lax.rem(place, 2)
    first = core == 0

    def phys(o):
        return jnp.where(first, o, blocks - 1 - o)

    def within(distance):
        return jnp.logical_and(place + distance >= 0, place + distance < places)

    sibling = place + 1 - 2 * core
    forth = jnp.where(first, -2, 2)

    def at(distance):
        return lax.rem(place + distance + places, places)

    sends_to = at(forth)
    gets_from = at(-forth)
    sends, gets = within(forth), within(-forth)
    gets_near = within(1)

    barrier = pltpu.get_barrier_semaphore()
    around = (-forth, forth, 1, -1)
    for d in around:

        @pl.when(within(d))
        def _():
            pl.semaphore_signal(
                barrier, inc=1, device_id={"blk": place + d}, device_id_type=MESH
            )

    for j in (2, 1, 3):
        pl.semaphore_signal(
            barrier, inc=1, device_id={"rep": lax.rem(y + j, REP)}, device_id_type=MESH
        )

    def piece_rows(i):
        _, start, size = parts[i]
        return pl.ds(pl.multiple_of(y * quarter + start, size), size)

    loads = []
    for i in range(count):
        o = parts[i][0]
        loads.append(
            pltpu.make_async_copy(
                emb.at[phys(o), piece_rows(i), :],
                stage.at[o, piece_rows(i), :],
                load_sem.at[i],
            )
        )
    rest = []
    for j in range(1, REP):
        span = pl.ds(pl.multiple_of(lax.rem(y + j, REP) * quarter, quarter), quarter)
        for o in range(blocks):
            rest.append((o, span))
            loads.append(
                pltpu.make_async_copy(
                    emb.at[phys(o), span, :],
                    stage.at[o, span, :],
                    load_sem.at[count + len(rest) - 1],
                )
            )
    pairs_load = pltpu.make_async_copy(pairs, pairs_there, pair_sem.at[0])
    pairs_load.start()
    for load in loads[:count]:
        load.start()
    pairs_load_s = pltpu.make_async_copy(pairs, pairs_here, pair_sem.at[1])
    pairs_load_s.start()

    row_max[...] = jnp.full(row_max.shape, -1.0, jnp.float32)
    msg_row[...] = jnp.full(msg_row.shape, -1.0, jnp.float32)


    @pl.when(jnp.logical_not(within(-1)))
    def _():
        got_near[...] = jnp.full(got_near.shape, -1.0, jnp.float32)

    @pl.when(jnp.logical_not(sends))
    def _():
        got_far[...] = jnp.full(got_far.shape, -1.0, jnp.float32)

    @pl.when(jnp.logical_not(within(-2)))
    def _():
        pairs_far[...] = jnp.zeros(pairs_far.shape, jnp.int32)

    neighbours = sum(within(d).astype(jnp.int32) for d in around)
    def unit(block):
        squares = jnp.sum(block * block, axis=1, keepdims=True)
        return (block * lax.rsqrt(squares + 1e-06)).astype(jnp.bfloat16)

    def part(i):
        _, start, size = parts[i]
        return pl.ds(start, size)

    def of_block(q):
        return [i for i in range(count) if parts[i][0] == q]

    def far_copy(i):
        return pltpu.make_async_remote_copy(
            src_ref=mine.at[parts[i][0], part(i), :],
            dst_ref=far.at[parts[i][0], part(i), :],
            send_sem=far_send.at[i],
            recv_sem=far_recv.at[i],
            device_id={"blk": sends_to},
            device_id_type=MESH,
        )

    def last_copy(i):
        return pltpu.make_async_remote_copy(
            src_ref=mine.at[parts[i][0], part(i), :],
            dst_ref=near.at[parts[i][0], part(i), :],
            send_sem=far_send.at[i],
            recv_sem=near_recv.at[i],
            device_id={"blk": at(-1)},
            device_id_type=MESH,
        )

    def to_sibling(i, source, target, send, recv):
        return pltpu.make_async_remote_copy(
            src_ref=source.at[parts[i][0], part(i), :],
            dst_ref=target.at[parts[i][0], part(i), :],
            send_sem=send.at[i],
            recv_sem=recv.at[i],
            device_id={"blk": sibling},
            device_id_type=MESH,
        )

    def near_copy(i):
        return to_sibling(i, mine, near, near_send, near_recv)

    def relay_copy(i):
        if i < last:
            return to_sibling(i, far, near, relay_send, near_recv)
        return to_sibling(i, near, far, relay_send, far_recv)

    pairs_copy = pltpu.make_async_remote_copy(
        src_ref=pairs_there,
        dst_ref=pairs_far,
        send_sem=pair_sem.at[2],
        recv_sem=pair_sem.at[3],
        device_id={"blk": at(2)},
        device_id_type=MESH,
    )
    last = of_block(blocks - 1)[0]
    for i in range(count):
        o = parts[i][0]
        loads[i].wait()
        if i == 1:
            for load in loads[count:]:
                load.start()
        value = unit(stage[o, piece_rows(i), :])
        mine[o, part(i), :] = value
        own[o, piece_rows(i), :] = value
        if i == 0:
            pairs_load.wait()
            pl.semaphore_wait(barrier, neighbours + REP - 1)

            @pl.when(within(2))
            def _():
                pairs_copy.start()

        if i < last:

            @pl.when(sends)
            def _():
                far_copy(i).start()

        else:

            @pl.when(jnp.logical_and(core == 0, sends))
            def _():
                last_copy(i).start()

            @pl.when(jnp.logical_and(core == 1, sends))
            def _():
                far_copy(i).start()

        @pl.when(core == 1)
        def _():
            near_copy(i).start()

    for d in around:

        @pl.when(within(d))
        def _():
            pl.semaphore_signal(
                group_sem, inc=1, device_id={"blk": place + d}, device_id_type=MESH
            )

    for n, (o, span) in enumerate(rest):
        loads[count + n].wait()
        own[o, span, :] = unit(stage[o, span, :])

    @pl.when(within(-2))
    def _():
        pairs_copy.wait_recv()

    pairs_move = pltpu.make_async_copy(pairs_far, pairs_far_s, pair_sem.at[4])
    pairs_move.start()
    pairs_load_s.wait()
    pairs_move.wait()

    def cap(listed):
        return listed.astype(jnp.float32) * 1e30 - 1.0

    def own_cap(o1, o2):
        return cap(pairs_here[jnp.where(first, o1, blocks - 1 - o2), o2 - o1 - 1])

    def near_cap(o, q):
        return cap(
            pairs_here[
                jnp.where(first, o, blocks - 1 - o),
                jnp.where(first, 2 * blocks - 2 - q - o, o + q),
            ]
        )

    def far_cap(o, q):
        here = pairs_here[o, 2 * blocks - 1 + q - o]
        there = pairs_far_s[blocks - 1 - q, 2 * blocks - 1 + q - o]
        return cap(jnp.where(first, here, there))

    def multiply(left, targets):
        kept = None
        for o, limit in targets:
            mine_max = None
            for c in range(rows // LANES):
                lanes = pl.ds(c * LANES, LANES)
                sim = lax.dot_general(
                    left, own[o, lanes, :], NT, preferred_element_type=jnp.float32
                )
                down = jnp.minimum(fold_rows(sim), limit)
                row_max[o, :, lanes] = jnp.maximum(row_max[o, :, lanes], down)
                across = fold_lanes(sim)
                mine_max = across if mine_max is None else jnp.maximum(mine_max, across)
            mine_max = jnp.minimum(mine_max, limit)
            kept = mine_max if kept is None else jnp.maximum(kept, mine_max)
        turned = [
            jnp.max(kept[128 * j : 128 * (j + 1), :].T, axis=0, keepdims=True)
            for j in range(quarter // 128)
        ]
        return jnp.concatenate(turned, axis=1)

    lanes_here = pl.ds(pl.multiple_of(y * quarter, quarter), quarter)
    for q in range(blocks - 1):
        targets = [(o, own_cap(q, o)) for o in range(q + 1, blocks)]
        msg_row[q, :, lanes_here] = multiply(mine[q], targets)

    def near_tiles(q):
        targets = [(o, near_cap(o, q)) for o in range(blocks)]
        msg_near[q] = multiply(near[q], targets)

    def far_tiles(q):
        targets = [(o, far_cap(o, q)) for o in range(q, blocks)]
        msg_far[q] = multiply(far[q], targets)

    def end_copy(k, source, target, recv, blk, rep):
        return pltpu.make_async_remote_copy(
            src_ref=source,
            dst_ref=target.at[y],
            send_sem=end_send.at[k],
            recv_sem=recv.at[y],
            device_id={"blk": blk, "rep": rep},
            device_id_type=MESH,
        )

    near_ends, far_ends, row_ends = [], [], []
    for j in (2, 1, 3, 0):
        rep = lax.rem(y + j, REP)
        near_ends.append(
            end_copy(3 * j, msg_near, got_near, got_near_recv, at(1), rep)
        )
        far_ends.append(
            end_copy(3 * j + 1, msg_far, got_far, got_far_recv, gets_from, rep)
        )
        if j:
            row_ends.append(
                end_copy(3 * j + 2, msg_row, got_row, row_recv, place, rep)
            )

    def fold(o):
        msg_row[o] = jnp.maximum(
            msg_row[o], jnp.max(row_max[o], axis=0, keepdims=True)
        )

    def relay(i):
        (far_copy(i) if i < last else near_copy(i)).wait_recv()
        relay_copy(i).start()

    for q in range(blocks - 1):
        pieces = of_block(q)
        half = len(pieces) // 2

        @pl.when(core == 0)
        def _():
            @pl.when(gets)
            def _():
                for i in pieces[:half]:
                    relay(i)

            for i in pieces:
                near_copy(i).wait_recv()
            near_tiles(q)

            @pl.when(gets)
            def _():
                for i in pieces[half:]:
                    relay(i)
                far_tiles(q)

        @pl.when(core == 1)
        def _():
            @pl.when(gets)
            def _():
                for i in pieces:
                    far_copy(i).wait_recv()
                far_tiles(q)

            @pl.when(gets_near)
            def _():
                for i in pieces:
                    near_copy(i).wait_recv()
                near_tiles(q)

    pl.semaphore_wait(group_sem, neighbours)

    @pl.when(gets_near)
    def _():
        @pl.when(core == 0)
        def _():
            for i in range(last, count):
                near_copy(i).wait_recv()

        @pl.when(core == 1)
        def _():
            for i in range(last, count):
                relay(i)

        near_tiles(blocks - 1)
        for copy in near_ends:
            copy.start()

    for o in range(blocks - 1):
        fold(o)

    @pl.when(gets)
    def _():
        for i in range(last, count):
            far_copy(i).wait_recv()
        far_tiles(blocks - 1)
        for copy in far_ends:
            copy.start()

    fold(blocks - 1)
    for copy in row_ends:
        copy.start()

    @pl.when(within(2))
    def _():
        pairs_copy.wait_send()

    @pl.when(sends)
    def _():
        for i in range(count):
            far_copy(i).wait_send()

    @pl.when(core == 1)
    def _():
        for i in range(count):
            near_copy(i).wait_send()

        @pl.when(gets_near)
        def _():
            for i in range(last, count):
                relay_copy(i).wait_send()

    @pl.when(jnp.logical_and(core == 0, gets))
    def _():
        for i in range(last):
            relay_copy(i).wait_send()

    for copy in row_ends:
        copy.wait_send()

    @pl.when(gets_near)
    def _():
        for copy in near_ends:
            copy.wait_send()

    @pl.when(gets)
    def _():
        for copy in far_ends:
            copy.wait_send()

    def arrived(source, target, recv, slot):
        pltpu.make_async_remote_copy(
            src_ref=source,
            dst_ref=target.at[slot],
            send_sem=end_send.at[0],
            recv_sem=recv.at[slot],
            device_id={"rep": lax.rem(y + 1, REP)},
            device_id_type=MESH,
        ).wait_recv()

    @pl.when(within(-1))
    def _():
        for j in range(REP):
            arrived(msg_near, got_near, got_near_recv, lax.rem(y + j, REP))

    best = []
    for o in range(blocks):
        side = [got_near[j, o] for j in range(REP)]
        best.append(jnp.maximum(msg_row[o], jnp.concatenate(side, axis=1)))
    for j in range(1, REP):
        arrived(msg_row, got_row, row_recv, lax.rem(y + j, REP))
    for o in range(blocks):
        for j in range(1, REP):
            best[o] = jnp.maximum(best[o], got_row[lax.rem(y + j, REP), o])

    @pl.when(sends)
    def _():
        for j in range(REP):
            arrived(msg_far, got_far, got_far_recv, lax.rem(y + j, REP))

    for o in range(blocks):
        side = [got_far[j, o] for j in range(REP)]
        best[o] = jnp.maximum(best[o], jnp.concatenate(side, axis=1))
    for o in range(blocks):
        out[o : o + 1, :] = jnp.where(first, best[o], best[blocks - 1 - o])


def solution(mesh):
    places = mesh.shape["blk"]

    def per_device(embeddings, pairs):
        blocks, rows, width = embeddings.shape
        reach = pairs.shape[1]
        quarter = rows // REP
        count = sum(len(cut) for cut in CUTS)
        dma = pltpu.SemaphoreType.DMA

        def body(*refs):
            kernel(places, *refs)

        return pl.pallas_call(
            body,
            out_shape=pltpu.VMEM((blocks, rows), jnp.float32),
            in_specs=[pl.BlockSpec(memory_space=pltpu.HBM)] * 2,
            out_specs=pl.BlockSpec(memory_space=pltpu.VMEM),
            scratch_shapes=[
                pltpu.VMEM((blocks, rows, width), jnp.float32),
                pltpu.VMEM((blocks, rows, width), jnp.bfloat16),
                pltpu.VMEM((blocks, quarter, width), jnp.bfloat16),
                pltpu.VMEM((blocks, quarter, width), jnp.bfloat16),
                pltpu.VMEM((blocks, quarter, width), jnp.bfloat16),
                pltpu.VMEM((blocks, 8, rows), jnp.float32),
                pltpu.SMEM((blocks, reach), jnp.int32),
                pltpu.VMEM((blocks, reach), jnp.int32),
                pltpu.VMEM((blocks, reach), jnp.int32),
                pltpu.SMEM((blocks, reach), jnp.int32),
                pltpu.VMEM((blocks, 1, rows), jnp.float32),
                pltpu.VMEM((blocks, 1, quarter), jnp.float32),
                pltpu.VMEM((blocks, 1, quarter), jnp.float32),
                pltpu.VMEM((REP, blocks, 1, rows), jnp.float32),
                pltpu.VMEM((REP, blocks, 1, quarter), jnp.float32),
                pltpu.VMEM((REP, blocks, 1, quarter), jnp.float32),
                dma((count + (REP - 1) * blocks,)),
                dma((5,)),
                dma((count,)),
                dma((count,)),
                dma((count,)),
                dma((count,)),
                dma((count,)),
                dma((3 * REP,)),
                dma((REP,)),
                dma((REP,)),
                dma((REP,)),
                pltpu.SemaphoreType.REGULAR,
            ],
            compiler_params=pltpu.CompilerParams(
                collective_id=0, has_side_effects=True, vmem_limit_bytes=56 << 20
            ),
            name="neighbours",
        )(embeddings, pairs)

    return jax.shard_map(
        per_device,
        mesh=mesh,
        in_specs=(P("blk", None, None), P("blk", None)),
        out_specs=P("blk", None),
        check_vma=False,
    )
```
